128 devices in a mesh: section: 8 (over y, core), ep: 16 (over z, x).
Axes of the slice: x: 4, y: 4, z: 4, core: 2. Of those that a mesh axis runs over, the one named last changes fastest.
Arguments:
- rows_in: bfloat16 [4, 128, 7168], P(None, 'ep'), may hold values from -6 to 6
- routes: int32 [8, 4, 128, 2], P('section', None, 'ep'), may hold values from 0 to 7, all different within a row; in each aligned block of 8 rows (0 to 7, 8 to 15, ..., all dimensions but the last counted through in order) at most 4 rows name the same one
- hot_blocks: int32 [8], P('section'), may hold values from 0 to 31
- gains: float32 [8, 7168], P('section'), may hold values from 0.1 to 1.9
- router: bfloat16 [8, 7168, 8], P('section'), may hold values from -0.0625 to 0.0625
- w_gate: bfloat16 [8, 7168, 8192], P('section', None, 'ep'), may hold values from -0.0625 to 0.0625
- w_up: bfloat16 [8, 7168, 8192], P('section', None, 'ep'), may hold values from -0.0625 to 0.0625
- w_down: bfloat16 [8, 8192, 7168], P('section', 'ep'), may hold values from -0.1875 to 0.1875
Outputs:
- section_rows: bfloat16 [8, 4, 128, 7168], P('section', None, 'ep')
- relative_load: float32 [8, 16], P('section', 'ep')
The draws below stay inside these ranges and needn't reach their ends.
Inputs may be any that keep to these rules, and one draw needn't show every extreme that they name: `routes`: in every layer and micro-batch the 8 rows of one device name each expert at most 4 times.
All inputs are finite; a program needn't handle non-finite values.
Results may differ from the reference program's by a relative error of at most 0.025.
Values may be sent and summed in bfloat16 or wider, within the bound.
No kernel may reach another device: no remote copies, remote signals or barrier semaphores. Data moves between devices by JAX's collectives and lax.ppermute only.
A program may use at most 128 MiB of HBM per device.

```python
import math
import jax
import jax.numpy as jnp
import numpy as np
from jax import lax

D = 7168
FFW = 1024
BLK = 256
TOP = 2
MICRO = 4
TOK_DEV = 8
CAP = 4
EXPERTS = 8
BLOCKS = 32
LAYERS = 8
TOKENS = 128
N_EP = 16


def touch_ends(result, key, least, top_value):
    longest = result.shape.index(max(result.shape))
    spots = []
    for shift in (0, 1):
        where = [jax.random.randint(jax.random.fold_in(key, axis), (), 0, length) for axis, length in enumerate(result.shape)]
        where[longest] = (where[longest] + shift) % result.shape[longest]
        spots.append(tuple(where))
    return result.at[spots[0]].set(least).at[spots[1]].set(top_value)


def level_of(own_key, extent, cuts, smallest, high):
    gain = 1.0
    for position, shards_of in cuts:
        draws = jax.random.uniform(jax.random.fold_in(jax.random.fold_in(own_key, 6), position), (shards_of,), jnp.float32, smallest / len(cuts), high / len(cuts))
        gain = gain * jnp.repeat(jnp.exp(draws), extent[position] // shards_of).reshape((-1,) + (1,) * (len(extent) - 1 - position))
    return gain


def deal_out(stream_key, own, number, rows, amount, top, limit, slope):
    ranking = jax.random.permutation(stream_key, amount)
    heavy_load, common = shares(amount, rows * top, limit, slope, True), shares(amount, rows * top, limit, slope, False)
    places = jnp.arange(amount)

    def named(lengths, turn):
        used = int((lengths > 0).sum())
        fixed = max(1, used // 4)
        moved = fixed + (places - fixed + turn * (used - fixed)) % max(1, amount - fixed)
        return jnp.zeros((amount,), jnp.int32).at[ranking[jnp.where(places < fixed, places, moved)]].set(jnp.asarray(lengths, jnp.int32))

    lengths = jnp.where(number % 4 == 0, named(heavy_load, number // 4), named(common, number - number // 4 - 1))
    mixed = jax.random.permutation(jax.random.fold_in(own, 3), amount)
    donor, sink = mixed[0:amount // 2 * 2:2], mixed[1:amount // 2 * 2:2]
    room = jnp.minimum(lengths[donor] - 1, limit - lengths[sink]) // 2
    room = jnp.where((donor == ranking[0]) | (sink == ranking[0]) | (lengths[sink] == 0), 0, jnp.maximum(room, 0))
    moved = jax.random.randint(jax.random.fold_in(own, 4), (amount // 2,), 0, 1 << 20) % (room + 1)
    lengths = lengths.at[donor].add(-moved).at[sink].add(moved)
    members = jnp.searchsorted(jnp.cumsum(lengths), jnp.arange(rows * top), side="right").astype(jnp.int32)
    table = members.reshape(top, rows).T
    table = table[jax.random.permutation(jax.random.fold_in(own, 1), rows)]
    turn = jax.random.randint(jax.random.fold_in(own, 2), (rows, 1), 0, top)
    return jnp.take_along_axis(table, (jnp.arange(top)[None, :] + turn) % top, axis=1)


def shares(number_of, total, bound, skew, full):
    weights = [(1 << 20) // math.isqrt(grade ** skew) + 1 for grade in range(1, number_of + 1)]
    largest = bound if full else min(bound, max(-(-total // number_of), total * weights[0] // sum(weights)))
    least = 1 if total - largest >= number_of - 1 else 0
    holding, spare = [largest] + [least] * (number_of - 1), total - largest - least * (number_of - 1)
    while spare > 0:
        candidates = [i for i in range(1, number_of) if holding[i] < largest] or [i for i in range(1, number_of) if holding[i] < bound]
        pool, left = sum([weights[i] for i in candidates]), spare
        for i in candidates:
            extra = min(bound - holding[i], max(1, left * weights[i] // pool), spare)
            holding[i] = holding[i] + extra
            spare = spare - extra
    return np.array(holding)


def scatter_about(stream_key, shape, deviation, most, split=(), kind=jnp.bfloat16):
    gain = level_of(stream_key, shape, split, -0.22, 0.18) if split else 1.0
    result = jax.random.normal(stream_key, shape, jnp.float32) * deviation * gain
    return jnp.minimum(jnp.maximum(result, -most), most).astype(kind)


def setup_inputs(seed: int = 0) -> dict:
    key_of = jax.random.split(jax.random.key(seed), 9)
    rows_in = scatter_about(key_of[0], (MICRO, TOKENS, D), 1.0, 6.0, ((1, 16),))
    routes_keys = jax.random.split(jax.random.fold_in(key_of[1], 1), LAYERS * MICRO * TOKENS // TOK_DEV)
    routes_turns = jax.random.permutation(jax.random.fold_in(key_of[1], 3), LAYERS * MICRO * TOKENS // TOK_DEV)
    routes = jax.vmap(lambda own, number: deal_out(jax.random.fold_in(key_of[1], 2), own, number, TOK_DEV, EXPERTS, TOP, CAP, 2))(routes_keys, routes_turns).reshape((LAYERS, MICRO, TOKENS, TOP))
    hot_blocks = touch_ends(jax.random.randint(key_of[2], (LAYERS,), 0, BLOCKS), jax.random.fold_in(key_of[2], 1), 0, BLOCKS - 1).astype(jnp.int32)
    gains = jnp.clip(1.0 + 0.18 * jax.random.normal(key_of[3], (LAYERS, D), jnp.float32), 0.1, 1.9)
    router = scatter_about(key_of[4], (LAYERS, D, EXPERTS), D ** -0.5, 0.0625, ((0, 8),))
    w_gate = scatter_about(key_of[5], (LAYERS, D, EXPERTS * FFW), D ** -0.5, 0.0625, ((0, 8), (2, 16)))
    w_up = scatter_about(key_of[6], (LAYERS, D, EXPERTS * FFW), D ** -0.5, 0.0625, ((0, 8), (2, 16)))
    w_down = scatter_about(key_of[7], (LAYERS, EXPERTS * FFW, D), FFW ** -0.5, 0.1875, ((0, 8), (1, 16)))
    return {"rows_in": rows_in, "routes": routes, "hot_blocks": hot_blocks, "gains": gains, "router": router, "w_gate": w_gate, "w_up": w_up, "w_down": w_down}


def apply_layer(rows, route_ids, hot_index, norm_gain, router_w, gate_w, up_w, down_w, down_float):
    rows_float = rows.astype(jnp.float32)
    mean_square = lax.optimization_barrier(jnp.mean(rows_float * rows_float, axis=-1, keepdims=True))
    normed = (rows_float * lax.rsqrt(mean_square + 1e-06) * norm_gain).astype(jnp.bfloat16)
    scores = jax.nn.sigmoid(jnp.dot(normed, router_w, preferred_element_type=jnp.float32))
    chosen = jnp.take_along_axis(scores, route_ids, axis=1)
    gate_weights = 2.5 * chosen / lax.optimization_barrier(jnp.sum(chosen, axis=1, keepdims=True))
    gate_value = jnp.dot(normed, gate_w, preferred_element_type=jnp.float32)
    up_value = jnp.dot(normed, up_w, preferred_element_type=jnp.float32)
    activation = (jax.nn.silu(gate_value) * up_value).astype(jnp.bfloat16)
    column_block = jnp.arange(EXPERTS * FFW, dtype=jnp.int32) // BLK
    home_act = jnp.where((column_block != hot_index)[None, :], activation, jnp.zeros_like(activation))
    token_count = rows.shape[0]
    home_part = jnp.einsum('tpc,pcd->tpd', home_act.reshape(token_count, N_EP, 2 * BLK).astype(jnp.float32), down_float)
    home_part = lax.optimization_barrier(home_part.astype(jnp.bfloat16)).astype(jnp.float32)
    halves = home_part.reshape(token_count, EXPERTS, 2, D)
    pair_sum = halves[:, :, 0, :] + halves[:, :, 1, :]
    hot_act = lax.dynamic_slice_in_dim(activation, (hot_index * BLK).astype(jnp.int32), BLK, 1)
    hot_down = lax.dynamic_slice_in_dim(down_w, (hot_index * BLK).astype(jnp.int32), BLK, 0)
    hot_part = jnp.dot(hot_act, hot_down, preferred_element_type=jnp.float32)
    hot_part = lax.optimization_barrier(hot_part.astype(jnp.bfloat16)).astype(jnp.float32)
    one_hot = (route_ids[:, :, None] == jnp.arange(EXPERTS, dtype=jnp.int32)[None, None, :]).astype(jnp.float32)
    selected = jnp.einsum('tke,ted->tkd', one_hot, pair_sum, precision=lax.Precision.HIGHEST)
    hot_expert = hot_index // (FFW // BLK)
    is_hot = (route_ids == hot_expert).astype(jnp.float32)[:, :, None]
    routed_sum = lax.optimization_barrier(jnp.sum(gate_weights[:, :, None] * (selected + is_hot * hot_part[:, None, :]), axis=1))
    return (rows_float + routed_sum).astype(jnp.bfloat16)

def layer_load(route_layer, hot_index):
    member = (route_layer[..., None] == jnp.arange(EXPERTS, dtype=jnp.int32)).astype(jnp.int32)
    expert_total = lax.optimization_barrier(jnp.sum(member, axis=(0, 1, 2)))
    device_ids = jnp.arange(N_EP, dtype=jnp.int32)
    home_units = expert_total[device_ids // 2] * (2 - (device_ids == hot_index // 2).astype(jnp.int32))
    hot_expert = hot_index // (FFW // BLK)
    per_token = lax.optimization_barrier(jnp.sum((route_layer == hot_expert).astype(jnp.int32), axis=(0, 2)))
    own_units = lax.optimization_barrier(jnp.sum(per_token.reshape(N_EP, TOK_DEV), axis=1))
    unit_count = (home_units + own_units).astype(jnp.float32)
    return unit_count / float(MICRO * TOK_DEV * TOP * (FFW // BLK))

def reference(rows_in, routes, hot_blocks, gains, router, w_gate, w_up, w_down):
    current = rows_in
    layer_rows = []
    load_rows = []
    for layer_index in range(LAYERS):
        down_float = w_down[layer_index].astype(jnp.float32).reshape(N_EP, 2 * BLK, D)
        hot_index = hot_blocks[layer_index]
        next_list = []
        for micro_index in range(MICRO):
            next_list.append(apply_layer(current[micro_index], routes[layer_index, micro_index], hot_index, gains[layer_index], router[layer_index], w_gate[layer_index], w_up[layer_index], w_down[layer_index], down_float))
        current = jnp.stack(next_list)
        layer_rows.append(current)
        load_rows.append(layer_load(routes[layer_index], hot_index))
    return (jnp.stack(layer_rows), jnp.stack(load_rows))
```

```python
import jax
import jax.numpy as jnp
from jax import lax
from jax.sharding import PartitionSpec as P

FFW = 1024
BLK = 256


def shifted(block, axis, distance):
    devices = range(lax.axis_size(axis))
    route = [(i - distance, i) for i in devices if i - distance in devices]
    return lax.ppermute(block, axis, route)


def local(rows_in, routes, hot_blocks, gains, router, w_gate, w_up, w_down):
    section_index = lax.axis_index("section")
    ep_index = lax.axis_index("ep")
    section_count = lax.axis_size("section")
    micro_count, tok_rows, model_width = rows_in.shape
    expert_count = router.shape[2]
    top_count = routes.shape[3]
    capacity = tok_rows // 2
    blocks_per_expert = FFW // BLK
    hot_index = hot_blocks[0]
    owner_index = hot_index // 2
    hot_expert = hot_index // blocks_per_expert
    expert_ids = lax.iota(jnp.int32, expert_count)

    member = (routes[0][:, :, :, None] == expert_ids).astype(jnp.float32)
    routed = jnp.sum(member, axis=2)
    before = (
        lax.broadcasted_iota(jnp.int32, (tok_rows, tok_rows), 0)
        > lax.broadcasted_iota(jnp.int32, (tok_rows, tok_rows), 1)
    ).astype(jnp.float32)
    slot_rank = jnp.einsum("ts,mse->mte", before, routed)
    slot_ids = lax.iota(jnp.float32, capacity)
    placement = routed.transpose(0, 2, 1)[:, :, None, :] * (
        slot_rank.transpose(0, 2, 1)[:, :, None, :] == slot_ids[None, None, :, None]
    ).astype(jnp.float32)
    placement = jnp.repeat(placement, 2, axis=1).reshape(
        micro_count, expert_count * 2 * capacity, tok_rows
    )

    expert_load = jnp.sum(routed, axis=(0, 1))
    expert_total = lax.psum(expert_load, "ep")
    mine = (expert_ids == ep_index // 2).astype(jnp.float32)
    hot_one = (expert_ids == hot_expert).astype(jnp.float32)
    unit_count = jnp.sum(expert_total * mine) * (
        2.0 - (owner_index == ep_index).astype(jnp.float32)
    ) + jnp.sum(expert_load * hot_one)
    relative = unit_count / float(micro_count * tok_rows * top_count * blocks_per_expert)

    norm_gain = gains[0]
    router_w = router[0]
    gate_w = w_gate[0]
    up_w = w_up[0]
    down_w = w_down[0]

    def apply_layer(layer_input, member_m, place_m):
        rows_float = layer_input.astype(jnp.float32)
        mean_square = jnp.mean(rows_float * rows_float, axis=-1, keepdims=True)
        normed = (rows_float * lax.rsqrt(mean_square + 1e-06) * norm_gain).astype(jnp.bfloat16)
        send = jnp.dot(
            place_m.astype(jnp.bfloat16), normed, preferred_element_type=jnp.float32
        ).astype(jnp.bfloat16)
        recv = lax.all_to_all(send, "ep", split_axis=0, concat_axis=0, tiled=True)
        scores = jax.nn.sigmoid(jnp.dot(normed, router_w, preferred_element_type=jnp.float32))
        chosen = jnp.sum(member_m * scores[:, None, :], axis=2)
        gate_weights = 2.5 * chosen / jnp.sum(chosen, axis=1, keepdims=True)
        token_gate = jnp.sum(member_m * gate_weights[:, :, None], axis=1)
        wide_gate = jnp.repeat(token_gate.T, 2 * capacity, axis=0)
        weighting = (place_m * wide_gate).T
        gate_value = jnp.dot(recv, gate_w, preferred_element_type=jnp.float32)
        up_value = jnp.dot(recv, up_w, preferred_element_type=jnp.float32)
        activation = (jax.nn.silu(gate_value) * up_value).astype(jnp.bfloat16)
        part = jnp.dot(activation, down_w, preferred_element_type=jnp.float32).astype(jnp.bfloat16)
        back = lax.all_to_all(part, "ep", split_axis=0, concat_axis=0, tiled=True)
        high = weighting.astype(jnp.bfloat16)
        low = (weighting - high.astype(jnp.float32)).astype(jnp.bfloat16)
        both = jnp.dot(
            jnp.concatenate([high, low]), back, preferred_element_type=jnp.float32
        )
        routed_sum = both[:tok_rows] + both[tok_rows:]
        return (rows_float + routed_sum).astype(jnp.bfloat16)

    incoming = jnp.zeros((tok_rows, model_width), jnp.bfloat16)
    ticks = []
    for tick_index in range(micro_count + section_count - 1):
        micro_index = jnp.clip(tick_index - section_index, 0, micro_count - 1)
        if tick_index < micro_count:
            layer_input = jnp.where(section_index == 0, rows_in[tick_index], incoming)
        else:
            layer_input = incoming
        member_m = lax.dynamic_index_in_dim(member, micro_index, 0, keepdims=False)
        place_m = lax.dynamic_index_in_dim(placement, micro_index, 0, keepdims=False)
        next_rows = apply_layer(layer_input, member_m, place_m)
        ticks.append(next_rows)
        if tick_index < micro_count + section_count - 2:
            incoming = shifted(next_rows, "section", 1)
    outputs = lax.dynamic_slice_in_dim(jnp.stack(ticks), section_index, micro_count, 0)
    return (outputs[None], relative.reshape(1, 1))


def solution(mesh):
    return jax.shard_map(
        local,
        mesh=mesh,
        in_specs=(
            P(None, "ep", None),
            P("section", None, "ep", None),
            P("section"),
            P("section", None),
            P("section", None, None),
            P("section", None, "ep"),
            P("section", None, "ep"),
            P("section", "ep", None),
        ),
        out_specs=(P("section", None, "ep", None), P("section", "ep")),
        check_vma=False,
    )
```

```python
import functools

import jax
import jax.numpy as jnp
from jax import lax
from jax.experimental import pallas as pl
from jax.experimental.pallas import tpu as pltpu
from jax.sharding import PartitionSpec as P

FFW = 1024
BLK = 256
VM = pl.BlockSpec(memory_space=pltpu.VMEM)
SM = pl.BlockSpec(memory_space=pltpu.SMEM)
F32 = jnp.float32
BF16 = jnp.bfloat16


def shifted(block, axis, distance):
    devices = range(lax.axis_size(axis))
    route = [(i - distance, i) for i in devices if i - distance in devices]
    return lax.ppermute(block, axis, route)


def pre_kernel(tick, place_ref, rows_ref, came_ref, gain_ref, router_ref, pack_ref, unpack_ref, routed_ref, extra_ref,
               send_ref, mix_ref, input_ref):
    micro_count = pack_ref.shape[0]
    section = place_ref[0]
    m = jnp.clip(tick - section, 0, micro_count - 1)
    half = rows_ref.shape[2] // 2
    if tick == 0:
        x = rows_ref[0]
        send_ref[:, half:] = extra_ref[...]
    elif tick < micro_count:
        x = jnp.where(section == 0, rows_ref[tick].astype(F32), came_ref[...].astype(F32)).astype(BF16)
    else:
        x = came_ref[...]
    input_ref[...] = x
    x = x.astype(F32)
    mean_square = jnp.mean(x * x, axis=-1, keepdims=True)
    normed = x * lax.rsqrt(mean_square + 1e-06) * gain_ref[...]
    halves = jnp.concatenate([normed[:, :half], normed[:, half:]], axis=0).astype(BF16)
    send_ref[:, :half] = jnp.dot(pack_ref[m], halves, preferred_element_type=F32).astype(BF16)
    logits = lax.dot_general(
        normed.astype(BF16), router_ref[...], (((1,), (1,)), ((), ())), preferred_element_type=F32
    )
    scores = routed_ref[m] / (1.0 + jnp.exp(-logits))
    gates = 2.5 * scores / jnp.sum(scores, axis=1, keepdims=True)
    experts = gates.shape[1]
    rows = send_ref.shape[0]
    owner = lax.broadcasted_iota(jnp.int32, (gates.shape[0], rows), 1) // (rows // experts)
    wide = jnp.zeros(owner.shape, F32)
    for e in range(experts):
        wide = jnp.where(owner == e, gates[:, e : e + 1], wide)
    mix = jnp.concatenate([wide, wide], axis=0) * unpack_ref[m]
    high = mix.astype(BF16)
    mix_ref[: mix.shape[0]] = high
    mix_ref[mix.shape[0] :] = (mix - high.astype(F32)).astype(BF16)


def expert_kernel(rows_ref, gate_ref, up_ref, down_ref, *rest):
    if len(rest) == 4:
        load_ref, out_ref, total_ref, act_ref = rest
        units = jnp.sum(rows_ref[:, out_ref.shape[1] :].astype(F32), axis=0, keepdims=True) * 0.125
        total_ref[...] = units * load_ref[0:1] + load_ref[1:2]
    else:
        out_ref, act_ref = rest
    count, half = out_ref.shape
    hidden = gate_ref.shape[1]
    left = rows_ref[:, :half]
    keep = lax.broadcasted_iota(jnp.int32, (count, 256), 0) % 8 < 4

    def joined(w_ref, cols):
        a = jnp.dot(left, w_ref[:half, cols], preferred_element_type=F32)
        b = jnp.dot(left, w_ref[half:, cols], preferred_element_type=F32)
        return a + pltpu.roll(b, count - 4, 0)

    for n in range(hidden // 256):
        cols = slice(n * 256, n * 256 + 256)
        g = joined(gate_ref, cols)
        u = joined(up_ref, cols)
        act = g / (1.0 + jnp.exp(-g)) * u
        act = jnp.where(keep, act, 0.0)
        act_ref[:, cols] = act.astype(BF16)
        act_ref[:, n * 256 + hidden : n * 256 + hidden + 256] = pltpu.roll(act, 4, 0).astype(BF16)
    first = act_ref[:, :hidden]
    second = act_ref[:, hidden:]
    wide = half // 2
    for n in range(2):
        cols = slice(n * wide, n * wide + wide)
        rest = slice(half + n * wide, half + n * wide + wide)
        out = jnp.dot(first, down_ref[:, cols], preferred_element_type=F32) + jnp.dot(
            second, down_ref[:, rest], preferred_element_type=F32
        )
        out_ref[:, cols] = out.astype(BF16)


def post_kernel(tick, place_ref, x_ref, back_ref, mix_ref, sofar_ref, out_ref, kept_ref):
    half = back_ref.shape[1]
    tokens = x_ref.shape[0]
    both = jnp.dot(mix_ref[...], back_ref[...], preferred_element_type=F32)
    total = both[: 2 * tokens] + both[2 * tokens :]
    x = x_ref[...].astype(F32)
    left = (x[:, :half] + total[:tokens]).astype(BF16)
    right = (x[:, half:] + total[tokens:]).astype(BF16)
    out_ref[:, :half] = left
    out_ref[:, half:] = right
    m = tick - place_ref[0]

    @pl.when((m >= 0) & (m < kept_ref.shape[0]))
    def _():
        kept_ref[m, :, :half] = left
        kept_ref[m, :, half:] = right


def local(rows_in, routes, hot_blocks, gains, router, w_gate, w_up, w_down):
    section_index = lax.axis_index("section")
    ep_index = lax.axis_index("ep")
    section_count = lax.axis_size("section")
    ep_count = lax.axis_size("ep")
    micro_count, tok_rows, model_width = rows_in.shape
    expert_count = router.shape[2]
    top_count = routes.shape[3]
    capacity = tok_rows // 2
    half = model_width // 2
    count = ep_count * 2 * capacity
    hidden = w_gate.shape[2]
    blocks_per_expert = FFW // BLK
    hot_index = hot_blocks[0]
    owner_index = hot_index // 2
    hot_expert = hot_index // blocks_per_expert
    expert_ids = lax.iota(jnp.int32, expert_count)

    member = (routes[0][:, :, :, None] == expert_ids).astype(F32)
    routed = jnp.sum(member, axis=2)
    before = (
        lax.broadcasted_iota(jnp.int32, (tok_rows, tok_rows), 0)
        > lax.broadcasted_iota(jnp.int32, (tok_rows, tok_rows), 1)
    ).astype(F32)
    slot_rank = jnp.einsum("ts,mse->mte", before, routed)
    slot_ids = lax.iota(F32, capacity)
    placement = routed[..., None] * (slot_rank[..., None] == slot_ids).astype(F32)
    halves = jnp.eye(2, dtype=F32)
    unpack = (
        placement[:, None, :, :, None, None, :]
        * halves[None, :, None, None, None, :, None]
        * jnp.ones((1, 1, 1, 1, 2, 1, 1), F32)
    ).reshape(micro_count, 2 * tok_rows, count)
    pack = unpack.transpose(0, 2, 1).astype(BF16)

    expert_load = jnp.sum(routed, axis=(0, 1))
    extra = jnp.broadcast_to(
        jnp.repeat(expert_load, 4 * capacity)[:, None], (count, 128)
    ).astype(BF16)
    hot_one = (expert_ids == hot_expert).astype(F32)
    mean_units = float(micro_count * tok_rows * top_count * blocks_per_expert)
    load_info = jnp.broadcast_to(
        jnp.stack(
            [2.0 - (owner_index == ep_index).astype(F32), jnp.sum(expert_load * hot_one)]
        )[:, None] / mean_units,
        (2, 128),
    )

    pack, unpack, routed, extra, load_info = lax.optimization_barrier(
        (pack, unpack, routed, extra, load_info)
    )
    router_t = router[0].T
    place = section_index.reshape(1)
    resident = functools.partial(pltpu.with_memory_space_constraint, memory_space=pltpu.VMEM)
    gate_w, up_w, down_w = resident(w_gate[0]), resident(w_up[0]), resident(w_down[0])
    row_shape = jax.ShapeDtypeStruct((tok_rows, model_width), BF16)

    def pre(tick, came):
        return pl.pallas_call(
            functools.partial(pre_kernel, tick),
            out_shape=(
                jax.ShapeDtypeStruct((count, half + (128 if tick == 0 else 0)), BF16),
                jax.ShapeDtypeStruct((4 * tok_rows, count), BF16),
                row_shape,
            ),
            in_specs=[SM] + [VM] * 8,
            out_specs=(VM, VM, VM),
            compiler_params=pltpu.CompilerParams(vmem_limit_bytes=8 << 20),
            name="pre",
        )(place, rows_in, came, gains, router_t, pack, unpack, routed, extra)

    def experts(rows, *load):
        out_shape = [jax.ShapeDtypeStruct((count, half), BF16)]
        out_shape += [jax.ShapeDtypeStruct((1, 128), F32) for _ in load]
        return pl.pallas_call(
            expert_kernel,
            out_shape=out_shape,
            in_specs=[VM] * (4 + len(load)),
            out_specs=[VM] * len(out_shape),
            scratch_shapes=[pltpu.VMEM((count, 2 * hidden), BF16)],
            compiler_params=pltpu.CompilerParams(vmem_limit_bytes=12 << 20),
            name="experts",
        )(rows, gate_w, up_w, down_w, *load)

    def post(tick, x, back, mix, kept):
        return pl.pallas_call(
            functools.partial(post_kernel, tick),
            out_shape=(row_shape, jax.ShapeDtypeStruct(kept.shape, kept.dtype)),
            in_specs=[SM] + [VM] * 4,
            out_specs=(VM, VM),
            input_output_aliases={4: 1},
            compiler_params=pltpu.CompilerParams(vmem_limit_bytes=8 << 20),
            name="post",
        )(place, x, back, mix, resident(kept))

    def exchange(block):
        return lax.all_to_all(block, "ep", split_axis=0, concat_axis=0, tiled=True)

    incoming = jnp.zeros((tok_rows, model_width), BF16)
    kept = jnp.zeros(rows_in.shape, BF16)
    last = micro_count + section_count - 2
    for tick in range(last + 1):
        send, mix, layer_input = pre(tick, incoming)
        received = exchange(send)
        if tick == 0:
            part, relative = experts(received, load_info)
        else:
            (part,) = experts(received)
        next_rows, kept = post(tick, layer_input, exchange(part), mix, kept)
        if tick < last:
            incoming = shifted(next_rows, "section", 1)
    return (kept[None], relative[:, :1])


def solution(mesh):
    return jax.shard_map(
        local,
        mesh=mesh,
        in_specs=(
            P(None, "ep", None),
            P("section", None, "ep", None),
            P("section"),
            P("section", None),
            P("section", None, None),
            P("section", None, "ep"),
            P("section", None, "ep"),
            P("section", "ep", None),
        ),
        out_specs=(P("section", None, "ep", None), P("section", "ep")),
        check_vma=False,
    )
```

```python
import functools

import jax
import jax.numpy as jnp
from jax import lax
from jax.experimental import pallas as pl
from jax.experimental.pallas import tpu as pltpu
from jax.sharding import PartitionSpec as P

FFW = 1024
BLK = 256
VM = pl.BlockSpec(memory_space=pltpu.VMEM)
SM = pl.BlockSpec(memory_space=pltpu.SMEM)
F32 = jnp.float32
BF16 = jnp.bfloat16


def live_hop(block, axis, tick, micro_count):
    last = lax.axis_size(axis) - 1
    route = [(s, s + 1) for s in range(last) if 0 <= tick - s < micro_count]
    return lax.ppermute(block, axis, route)


def row_ids(rows, lanes, experts, capacity):
    row = lax.broadcasted_iota(jnp.int32, (rows, lanes), 1)
    return row // (lanes // experts), row // capacity % 2, row % capacity


def column(routes, k):
    tokens = routes.shape[1]
    shape = (tokens, tokens)
    same = lax.broadcasted_iota(jnp.int32, shape, 0) == lax.broadcasted_iota(jnp.int32, shape, 1)
    spread = jnp.broadcast_to(routes[k : k + 1].astype(F32), shape)
    return jnp.sum(jnp.where(same, spread, 0.0), axis=1, keepdims=True)


def plan(hot_ref, routes_ref, unpack_ref, info_ref):
    micro_count, top_count, tokens = routes_ref.shape
    lanes = unpack_ref.shape[2]
    expert, half_id, slot = row_ids(tokens, lanes, 8, tokens // 2)
    before = (
        lax.broadcasted_iota(jnp.int32, (tokens, tokens), 0)
        > lax.broadcasted_iota(jnp.int32, (tokens, tokens), 1)
    ).astype(BF16)
    counts = jnp.zeros((tokens, lanes), F32)
    for m in range(micro_count):
        ids = routes_ref[m]
        hit = jnp.zeros((tokens, lanes), F32)
        for k in range(top_count):
            hit = hit + (column(ids, k) == expert.astype(F32)).astype(F32)
        rank = jnp.dot(before, hit.astype(BF16), preferred_element_type=F32)
        placed = jnp.where(rank == slot.astype(F32), hit, 0.0)
        unpack_ref[m, :tokens] = jnp.where(half_id == 0, placed, 0.0)
        unpack_ref[m, tokens:] = jnp.where(half_id == 1, placed, 0.0)
        counts = counts + hit
    counts = jnp.sum(counts, axis=0, keepdims=True)
    hot = hot_ref[0]
    device = lax.axis_index("ep")
    lane = lax.broadcasted_iota(jnp.int32, counts.shape, 1)
    per = lanes // 8
    homes = 2.0 - (hot // 2 == device).astype(F32)
    info_ref[0:1] = jnp.where(lane == device // 2 * per, homes, 0.0)
    info_ref[1:2] = jnp.where(lane == hot // (FFW // BLK) * per, counts, 0.0)
    return counts


def pre_kernel(tick, *refs):
    if tick == 0:
        hot_ref, *sources, send_ref, mix_ref, input_ref, unpack_ref, info_ref = refs[:10]
        rows_ref, gain_ref, router_ref, routes_ref, sems = refs[10:]
        copies = [
            pltpu.make_async_copy(source, held, sems.at[i])
            for i, (source, held) in enumerate(zip(sources, refs[10:14]))
        ]
        for copy in copies:
            copy.start()
        for copy in copies:
            copy.wait()
    else:
        rows_ref, gain_ref, router_ref, routes_ref, unpack_ref, came_ref, send_ref, mix_ref, input_ref = refs
    micro_count, tokens, width = rows_ref.shape
    half = width // 2
    section = lax.axis_index("section")
    m = jnp.clip(tick - section, 0, micro_count - 1)
    if tick == 0:
        counts = plan(hot_ref, routes_ref, unpack_ref, info_ref)
        send_ref[:, half:] = jnp.broadcast_to(
            counts, (send_ref.shape[0], counts.shape[1])
        ).astype(BF16)
        x = rows_ref[0]
    else:
        x = came_ref[...]
        if tick < micro_count:
            x = jnp.where(section == 0, rows_ref[tick].astype(F32), x.astype(F32)).astype(BF16)
    input_ref[...] = x
    x = x.astype(F32)
    mean_square = jnp.mean(x * x, axis=-1, keepdims=True)
    normed = x * lax.rsqrt(mean_square + 1e-06) * gain_ref[...]
    halves = jnp.concatenate([normed[:, :half], normed[:, half:]], axis=0).astype(BF16)
    unpack = unpack_ref[m]
    send_ref[:, :half] = lax.dot_general(
        unpack.astype(BF16), halves, (((0,), (0,)), ((), ())), preferred_element_type=F32
    ).astype(BF16)
    logits = lax.dot_general(
        normed.astype(BF16), router_ref[...], (((1,), (1,)), ((), ())), preferred_element_type=F32
    )
    experts = router_ref.shape[0]
    ids = routes_ref[m]
    expert = lax.broadcasted_iota(jnp.int32, (tokens, experts), 1)
    routed = jnp.zeros((tokens, experts), F32)
    for k in range(ids.shape[0]):
        routed = routed + (column(ids, k) == expert.astype(F32)).astype(F32)
    scores = routed / (1.0 + jnp.exp(-logits))
    gates = 2.5 * scores / jnp.sum(scores, axis=1, keepdims=True)
    owner = row_ids(tokens, unpack.shape[1], experts, tokens // 2)[0]
    wide = jnp.zeros(owner.shape, F32)
    for e in range(experts):
        wide = jnp.where(owner == e, gates[:, e : e + 1], wide)
    mix = jnp.concatenate([wide, wide], axis=0) * unpack
    high = mix.astype(BF16)
    mix_ref[: mix.shape[0]] = high
    mix_ref[mix.shape[0] :] = (mix - high.astype(F32)).astype(BF16)


def product(rows_ref, gate_ref, up_ref, down_ref, out_ref, act_ref, arrived):
    count, half = out_ref.shape
    hidden = gate_ref.shape[1]
    left = rows_ref[:, :half]
    keep = lax.broadcasted_iota(jnp.int32, (count, 256), 0) % 8 < 4

    def joined(w_ref, cols):
        a = jnp.dot(left, w_ref[:half, cols], preferred_element_type=F32)
        b = jnp.dot(left, w_ref[half:, cols], preferred_element_type=F32)
        return a + pltpu.roll(b, count - 4, 0)

    for n in range(hidden // 256):
        cols = slice(n * 256, n * 256 + 256)
        arrived(2 * n)
        g = joined(gate_ref, cols)
        arrived(2 * n + 1)
        u = joined(up_ref, cols)
        act = g / (1.0 + jnp.exp(-g)) * u
        act = jnp.where(keep, act, 0.0)
        act_ref[:, cols] = act.astype(BF16)
        act_ref[:, n * 256 + hidden : n * 256 + hidden + 256] = pltpu.roll(act, 4, 0).astype(BF16)
    first = act_ref[:, :hidden]
    second = act_ref[:, hidden:]
    wide = half // 2
    for n in range(2):
        cols = slice(n * wide, n * wide + wide)
        rest = slice(half + n * wide, half + n * wide + wide)
        arrived(hidden // 128 + n)
        out = jnp.dot(first, down_ref[:, cols], preferred_element_type=F32) + jnp.dot(
            second, down_ref[:, rest], preferred_element_type=F32
        )
        out_ref[:, cols] = out.astype(BF16)


def expert_kernel(rows_ref, gate_ref, up_ref, down_ref, out_ref, act_ref):
    product(rows_ref, gate_ref, up_ref, down_ref, out_ref, act_ref, lambda step: None)


def first_kernel(info_ref, rows_ref, gate_hbm, up_hbm, down_hbm,
                 out_ref, load_ref, gate_ref, up_ref, down_ref, act_ref, sems):
    half = out_ref.shape[1]
    hidden = gate_ref.shape[1]
    wide = half // 2
    steps = []
    for n in range(hidden // 256):
        cols = slice(n * 256, n * 256 + 256)
        steps.append([(gate_hbm, gate_ref, cols)])
        steps.append([(up_hbm, up_ref, cols)])
    for n in range(2):
        steps.append(
            [(down_hbm, down_ref, slice(c + n * wide, c + n * wide + wide)) for c in (0, half)]
        )
    copies = []
    for step in steps:
        started = []
        for src, dst, cols in step:
            index = sum(map(len, copies)) + len(started)
            copy = pltpu.make_async_copy(src.at[:, cols], dst.at[:, cols], sems.at[index])
            copy.start()
            started.append(copy)
        copies.append(started)

    units = jnp.sum(rows_ref[:, half:].astype(F32), axis=0, keepdims=True) * 0.125
    load_ref[...] = jnp.broadcast_to(
        jnp.sum(units * info_ref[0:1] + info_ref[1:2], axis=1, keepdims=True) / 256.0, load_ref.shape
    )

    def arrived(step):
        for copy in copies[step]:
            copy.wait()

    product(rows_ref, gate_ref, up_ref, down_ref, out_ref, act_ref, arrived)


def post_kernel(tick, x_ref, back_ref, mix_ref, *rest):
    out_ref, kept_ref = rest[-2:]
    half = back_ref.shape[1]
    tokens = x_ref.shape[0]
    both = jnp.dot(mix_ref[...], back_ref[...], preferred_element_type=F32)
    total = both[: 2 * tokens] + both[2 * tokens :]
    x = x_ref[...].astype(F32)
    left = (x[:, :half] + total[:tokens]).astype(BF16)
    right = (x[:, half:] + total[tokens:]).astype(BF16)
    out_ref[:, :half] = left
    out_ref[:, half:] = right
    m = tick - lax.axis_index("section")

    @pl.when((m >= 0) & (m < kept_ref.shape[0]))
    def _():
        kept_ref[m, :, :half] = left
        kept_ref[m, :, half:] = right


def local(rows_in, routes, hot_blocks, gains, router, w_gate, w_up, w_down):
    section_count = lax.axis_size("section")
    ep_count = lax.axis_size("ep")
    micro_count, tok_rows, model_width = rows_in.shape
    half = model_width // 2
    count = ep_count * tok_rows
    hidden = w_gate.shape[2]
    resident = functools.partial(pltpu.with_memory_space_constraint, memory_space=pltpu.VMEM)
    outside = functools.partial(pltpu.with_memory_space_constraint, memory_space=pltpu.HBM)
    HB = pl.BlockSpec(memory_space=pltpu.HBM)
    router_t = router[0].T
    routes_t = routes[0].transpose(0, 2, 1)
    row_shape = jax.ShapeDtypeStruct((tok_rows, model_width), BF16)

    def params(mib):
        return pltpu.CompilerParams(vmem_limit_bytes=mib << 20)

    def pre(tick, *more):
        out_shape = [
            jax.ShapeDtypeStruct((count, half + (count if tick == 0 else 0)), BF16),
            jax.ShapeDtypeStruct((4 * tok_rows, count), BF16),
            row_shape,
        ]
        if tick == 0:
            out_shape += [
                jax.ShapeDtypeStruct((micro_count, 2 * tok_rows, count), F32),
                jax.ShapeDtypeStruct((2, count), F32),
            ]
        values = (rows_in, gains, router_t, routes_t)
        if tick == 0:
            values = (hot_blocks, *map(outside, values))
            specs = [SM] + [HB] * 4
            scratch = [pltpu.VMEM(v.shape, v.dtype) for v in values[1:]]
            scratch += [pltpu.SemaphoreType.DMA((4,))]
        else:
            values += more
            specs = [VM] * len(values)
            scratch = []
        return pl.pallas_call(
            functools.partial(pre_kernel, tick),
            out_shape=out_shape,
            in_specs=specs,
            out_specs=[VM] * len(out_shape),
            scratch_shapes=scratch,
            compiler_params=params(8),
            name="pre",
        )(*values)

    part_shape = jax.ShapeDtypeStruct((count, half), BF16)
    act_shape = pltpu.VMEM((count, 2 * hidden), BF16)
    weights = (w_gate[0], w_up[0], w_down[0])

    def first(rows, info):
        return pl.pallas_call(
            first_kernel,
            out_shape=[part_shape, jax.ShapeDtypeStruct((1, 128), F32)]
            + [pltpu.VMEM(w.shape, w.dtype) for w in weights],
            in_specs=[VM, VM] + [HB] * 3,
            out_specs=[VM] * 5,
            scratch_shapes=[act_shape, pltpu.SemaphoreType.DMA((8,))],
            compiler_params=params(12),
            name="first",
        )(info, rows, *map(outside, weights))

    def experts(rows, held):
        return pl.pallas_call(
            expert_kernel,
            out_shape=part_shape,
            in_specs=[VM] * 4,
            out_specs=VM,
            scratch_shapes=[act_shape],
            compiler_params=params(12),
            name="experts",
        )(rows, *map(resident, held))

    def post(tick, x, back, mix, *kept):
        return pl.pallas_call(
            functools.partial(post_kernel, tick),
            out_shape=(row_shape, pltpu.VMEM(rows_in.shape, BF16)),
            in_specs=[VM] * (3 + len(kept)),
            out_specs=(VM, VM),
            input_output_aliases={3: 1} if kept else {},
            compiler_params=params(8),
            name="post",
        )(x, back, mix, *map(resident, kept))

    def exchange(block):
        return lax.all_to_all(block, "ep", split_axis=0, concat_axis=0, tiled=True)

    kept = ()
    last = micro_count + section_count - 2
    for tick in range(last + 1):
        if tick == 0:
            send, mix, layer_input, unpack, info = pre(tick)
            part, relative, *held = first(exchange(send), info)
        else:
            send, mix, layer_input = pre(tick, unpack, incoming)
            part = experts(exchange(send), held)
        next_rows, *kept = post(tick, layer_input, exchange(part), mix, *kept)
        if tick < last:
            incoming = live_hop(next_rows, "section", tick, micro_count)
    return (kept[0][None], relative[:, :1])


def solution(mesh):
    return jax.shard_map(
        local,
        mesh=mesh,
        in_specs=(
            P(None, "ep", None),
            P("section", None, "ep", None),
            P("section"),
            P("section", None),
            P("section", None, None),
            P("section", None, "ep"),
            P("section", None, "ep"),
            P("section", "ep", None),
        ),
        out_specs=(P("section", None, "ep", None), P("section", "ep")),
        check_vma=False,
    )
```

```python
import functools

import jax
import jax.numpy as jnp
from jax import lax
from jax.experimental import pallas as pl
from jax.experimental.pallas import tpu as pltpu
from jax.sharding import PartitionSpec as P

FFW = 1024
BLK = 256
VM = pl.BlockSpec(memory_space=pltpu.VMEM)
SM = pl.BlockSpec(memory_space=pltpu.SMEM)
F32 = jnp.float32
BF16 = jnp.bfloat16


def live_hop(block, axis, tick, micro_count):
    last = lax.axis_size(axis) - 1
    route = [(s, s + 1) for s in range(last) if 0 <= tick - s < micro_count]
    return lax.ppermute(block, axis, route)


PACE = 1


def pacing(token, tick, micro_count):
    last = lax.axis_size("section") - 1
    done = tick + 1 - micro_count
    sections = [0] if tick + 1 < micro_count else [done] if done % 2 == 0 and done < last else []
    n = lax.axis_size("ep")
    pairs = [(s * n + p, s * n + (p ^ 1)) for s in sections for p in range(n)]
    for _ in range(PACE if pairs else 0):
        token = lax.ppermute(token, ("section", "ep"), pairs)
    return (token,) if pairs else ()


def row_ids(rows, lanes, experts, capacity):
    row = lax.broadcasted_iota(jnp.int32, (rows, lanes), 1)
    return row // (lanes // experts), row // capacity % 2, row % capacity


def column(routes, k):
    tokens = routes.shape[1]
    shape = (tokens, tokens)
    same = lax.broadcasted_iota(jnp.int32, shape, 0) == lax.broadcasted_iota(jnp.int32, shape, 1)
    spread = jnp.broadcast_to(routes[k : k + 1].astype(F32), shape)
    return jnp.sum(jnp.where(same, spread, 0.0), axis=1, keepdims=True)


def plan(hot_ref, routes_ref, unpack_ref, info_ref):
    micro_count, top_count, tokens = routes_ref.shape
    lanes = unpack_ref.shape[2]
    expert, half_id, slot = row_ids(tokens, lanes, 8, tokens // 2)
    before = (
        lax.broadcasted_iota(jnp.int32, (tokens, tokens), 0)
        > lax.broadcasted_iota(jnp.int32, (tokens, tokens), 1)
    ).astype(BF16)
    counts = jnp.zeros((tokens, lanes), F32)
    for m in range(micro_count):
        ids = routes_ref[m]
        hit = jnp.zeros((tokens, lanes), F32)
        for k in range(top_count):
            hit = hit + (column(ids, k) == expert.astype(F32)).astype(F32)
        rank = jnp.dot(before, hit.astype(BF16), preferred_element_type=F32)
        placed = jnp.where(rank == slot.astype(F32), hit, 0.0)
        unpack_ref[m, :tokens] = jnp.where(half_id == 0, placed, 0.0)
        unpack_ref[m, tokens:] = jnp.where(half_id == 1, placed, 0.0)
        counts = counts + hit
    counts = jnp.sum(counts, axis=0, keepdims=True)
    hot = hot_ref[0]
    device = lax.axis_index("ep")
    lane = lax.broadcasted_iota(jnp.int32, counts.shape, 1)
    per = lanes // 8
    homes = 2.0 - (hot // 2 == device).astype(F32)
    info_ref[0:1] = jnp.where(lane == device // 2 * per, homes, 0.0)
    info_ref[1:2] = jnp.where(lane == hot // (FFW // BLK) * per, counts, 0.0)
    return counts


def pre_kernel(tick, *refs):
    if tick == 0:
        hot_ref, *sources, send_ref, mix_ref, input_ref, unpack_ref, info_ref = refs[:10]
        rows_ref, gain_ref, router_ref, routes_ref, sems = refs[10:]
        copies = [
            pltpu.make_async_copy(source, held, sems.at[i])
            for i, (source, held) in enumerate(zip(sources, refs[10:14]))
        ]
        for copy in copies:
            copy.start()
        for copy in copies:
            copy.wait()
    else:
        rows_ref, gain_ref, router_ref, routes_ref, unpack_ref, came_ref, *_, send_ref, mix_ref, input_ref = refs
    micro_count, tokens, width = rows_ref.shape
    half = width // 2
    section = lax.axis_index("section")
    m = jnp.clip(tick - section, 0, micro_count - 1)
    if tick == 0:
        counts = plan(hot_ref, routes_ref, unpack_ref, info_ref)
        send_ref[:, half:] = jnp.broadcast_to(
            counts, (send_ref.shape[0], counts.shape[1])
        ).astype(BF16)
        x = rows_ref[0]
    else:
        x = came_ref[...]
        if tick < micro_count:
            x = jnp.where(section == 0, rows_ref[tick].astype(F32), x.astype(F32)).astype(BF16)
    input_ref[...] = x
    x = x.astype(F32)
    mean_square = jnp.mean(x * x, axis=-1, keepdims=True)
    normed = x * lax.rsqrt(mean_square + 1e-06) * gain_ref[...]
    halves = jnp.concatenate([normed[:, :half], normed[:, half:]], axis=0).astype(BF16)
    unpack = unpack_ref[m]
    send_ref[:, :half] = lax.dot_general(
        unpack.astype(BF16), halves, (((0,), (0,)), ((), ())), preferred_element_type=F32
    ).astype(BF16)
    logits = lax.dot_general(
        normed.astype(BF16), router_ref[...], (((1,), (1,)), ((), ())), preferred_element_type=F32
    )
    experts = router_ref.shape[0]
    ids = routes_ref[m]
    expert = lax.broadcasted_iota(jnp.int32, (tokens, experts), 1)
    routed = jnp.zeros((tokens, experts), F32)
    for k in range(ids.shape[0]):
        routed = routed + (column(ids, k) == expert.astype(F32)).astype(F32)
    scores = routed / (1.0 + jnp.exp(-logits))
    gates = 2.5 * scores / jnp.sum(scores, axis=1, keepdims=True)
    owner = row_ids(tokens, unpack.shape[1], experts, tokens // 2)[0]
    wide = jnp.zeros(owner.shape, F32)
    for e in range(experts):
        wide = jnp.where(owner == e, gates[:, e : e + 1], wide)
    mix = jnp.concatenate([wide, wide], axis=0) * unpack
    high = mix.astype(BF16)
    mix_ref[: mix.shape[0]] = high
    mix_ref[mix.shape[0] :] = (mix - high.astype(F32)).astype(BF16)


def product(rows_ref, gate_ref, up_ref, down_ref, out_ref, act_ref, arrived):
    count, half = out_ref.shape
    hidden = gate_ref.shape[1]
    left = rows_ref[:, :half]
    keep = lax.broadcasted_iota(jnp.int32, (count, 256), 0) % 8 < 4

    def joined(w_ref, cols):
        a = jnp.dot(left, w_ref[:half, cols], preferred_element_type=F32)
        b = jnp.dot(left, w_ref[half:, cols], preferred_element_type=F32)
        return a + pltpu.roll(b, count - 4, 0)

    for n in range(hidden // 256):
        cols = slice(n * 256, n * 256 + 256)
        arrived(2 * n)
        g = joined(gate_ref, cols)
        arrived(2 * n + 1)
        u = joined(up_ref, cols)
        act = g / (1.0 + jnp.exp(-g)) * u
        act = jnp.where(keep, act, 0.0)
        act_ref[:, cols] = act.astype(BF16)
        act_ref[:, n * 256 + hidden : n * 256 + hidden + 256] = pltpu.roll(act, 4, 0).astype(BF16)
    first = act_ref[:, :hidden]
    second = act_ref[:, hidden:]
    wide = half // 2
    for n in range(2):
        cols = slice(n * wide, n * wide + wide)
        rest = slice(half + n * wide, half + n * wide + wide)
        arrived(hidden // 128 + n)
        out = jnp.dot(first, down_ref[:, cols], preferred_element_type=F32) + jnp.dot(
            second, down_ref[:, rest], preferred_element_type=F32
        )
        out_ref[:, cols] = out.astype(BF16)


def busy(tick, micro_count):
    m = tick - lax.axis_index("section")
    return (m >= 0) & (m <= micro_count)


def expert_kernel(tick, micro_count, rows_ref, gate_ref, up_ref, down_ref, out_ref, act_ref):
    @pl.when(busy(tick, micro_count))
    def _():
        product(rows_ref, gate_ref, up_ref, down_ref, out_ref, act_ref, lambda step: None)


def first_kernel(info_ref, rows_ref, gate_hbm, up_hbm, down_hbm,
                 out_ref, load_ref, gate_ref, up_ref, down_ref, act_ref, sems):
    half = out_ref.shape[1]
    hidden = gate_ref.shape[1]
    wide = half // 2
    steps = []
    for n in range(hidden // 256):
        cols = slice(n * 256, n * 256 + 256)
        steps.append([(gate_hbm, gate_ref, cols)])
        steps.append([(up_hbm, up_ref, cols)])
    for n in range(2):
        steps.append(
            [(down_hbm, down_ref, slice(c + n * wide, c + n * wide + wide)) for c in (0, half)]
        )
    copies = []
    for step in steps:
        started = []
        for src, dst, cols in step:
            index = sum(map(len, copies)) + len(started)
            copy = pltpu.make_async_copy(src.at[:, cols], dst.at[:, cols], sems.at[index])
            copy.start()
            started.append(copy)
        copies.append(started)

    units = jnp.sum(rows_ref[:, half:].astype(F32), axis=0, keepdims=True) * 0.125
    load_ref[...] = jnp.broadcast_to(
        jnp.sum(units * info_ref[0:1] + info_ref[1:2], axis=1, keepdims=True) / 256.0, load_ref.shape
    )

    def arrived(step):
        for copy in copies[step]:
            copy.wait()

    product(rows_ref, gate_ref, up_ref, down_ref, out_ref, act_ref, arrived)


def post_kernel(tick, x_ref, back_ref, mix_ref, *rest):
    out_ref, kept_ref = rest[-2:]
    half = back_ref.shape[1]
    tokens = x_ref.shape[0]
    both = jnp.dot(mix_ref[...], back_ref[...], preferred_element_type=F32)
    total = both[: 2 * tokens] + both[2 * tokens :]
    x = x_ref[...].astype(F32)
    left = (x[:, :half] + total[:tokens]).astype(BF16)
    right = (x[:, half:] + total[tokens:]).astype(BF16)
    out_ref[:, :half] = left
    out_ref[:, half:] = right
    m = tick - lax.axis_index("section")

    @pl.when((m >= 0) & (m < kept_ref.shape[0]))
    def _():
        kept_ref[m, :, :half] = left
        kept_ref[m, :, half:] = right


def local(rows_in, routes, hot_blocks, gains, router, w_gate, w_up, w_down):
    section_count = lax.axis_size("section")
    ep_count = lax.axis_size("ep")
    micro_count, tok_rows, model_width = rows_in.shape
    half = model_width // 2
    count = ep_count * tok_rows
    hidden = w_gate.shape[2]
    resident = functools.partial(pltpu.with_memory_space_constraint, memory_space=pltpu.VMEM)
    outside = functools.partial(pltpu.with_memory_space_constraint, memory_space=pltpu.HBM)
    HB = pl.BlockSpec(memory_space=pltpu.HBM)
    router_t = router[0].T
    routes_t = routes[0].transpose(0, 2, 1)
    row_shape = jax.ShapeDtypeStruct((tok_rows, model_width), BF16)

    def params(mib):
        return pltpu.CompilerParams(vmem_limit_bytes=mib << 20)

    def pre(tick, *more):
        out_shape = [
            jax.ShapeDtypeStruct((count, half + (count if tick == 0 else 0)), BF16),
            jax.ShapeDtypeStruct((4 * tok_rows, count), BF16),
            row_shape,
        ]
        if tick == 0:
            out_shape += [
                jax.ShapeDtypeStruct((micro_count, 2 * tok_rows, count), F32),
                jax.ShapeDtypeStruct((2, count), F32),
            ]
        values = (rows_in, gains, router_t, routes_t)
        if tick == 0:
            values = (hot_blocks, *map(outside, values))
            specs = [SM] + [HB] * 4
            scratch = [pltpu.VMEM(v.shape, v.dtype) for v in values[1:]]
            scratch += [pltpu.SemaphoreType.DMA((4,))]
        else:
            values += more
            specs = [VM] * len(values)
            scratch = []
        return pl.pallas_call(
            functools.partial(pre_kernel, tick),
            out_shape=out_shape,
            in_specs=specs,
            out_specs=[VM] * len(out_shape),
            scratch_shapes=scratch,
            compiler_params=params(8),
            name="pre",
        )(*values)

    part_shape = jax.ShapeDtypeStruct((count, half), BF16)
    act_shape = pltpu.VMEM((count, 2 * hidden), BF16)
    weights = (w_gate[0], w_up[0], w_down[0])

    def first(rows, info):
        return pl.pallas_call(
            first_kernel,
            out_shape=[part_shape, jax.ShapeDtypeStruct((1, 128), F32)]
            + [pltpu.VMEM(w.shape, w.dtype) for w in weights],
            in_specs=[VM, VM] + [HB] * 3,
            out_specs=[VM] * 5,
            scratch_shapes=[act_shape, pltpu.SemaphoreType.DMA((8,))],
            compiler_params=params(12),
            name="first",
        )(info, rows, *map(outside, weights))

    def experts(tick, rows, held):
        return pl.pallas_call(
            functools.partial(expert_kernel, tick, micro_count),
            out_shape=part_shape,
            in_specs=[VM] * 4,
            out_specs=VM,
            scratch_shapes=[act_shape],
            compiler_params=params(12),
            name="experts",
        )(rows, *map(resident, held))

    def post(tick, x, back, mix, *kept):
        return pl.pallas_call(
            functools.partial(post_kernel, tick),
            out_shape=(row_shape, pltpu.VMEM(rows_in.shape, BF16)),
            in_specs=[VM] * (3 + len(kept)),
            out_specs=(VM, VM),
            input_output_aliases={3: 1} if kept else {},
            compiler_params=params(8),
            name="post",
        )(x, back, mix, *map(resident, kept))

    def exchange(block):
        return lax.all_to_all(block, "ep", split_axis=0, concat_axis=0, tiled=True)

    kept = ()
    last = micro_count + section_count - 2
    for tick in range(last + 1):
        if tick == 0:
            send, mix, layer_input, unpack, info = pre(tick)
            part, relative, *held = first(exchange(send), info)
        else:
            send, mix, layer_input = pre(tick, unpack, incoming, *pace)
            part = experts(tick, exchange(send), held)
        next_rows, *kept = post(tick, layer_input, exchange(part), mix, *kept)
        if tick < last:
            incoming = live_hop(next_rows, "section", tick, micro_count)
            incoming, token = lax.optimization_barrier((incoming, mix))
            pace = pacing(token, tick, micro_count)
    return (kept[0][None], relative[:, :1])


def solution(mesh):
    return jax.shard_map(
        local,
        mesh=mesh,
        in_specs=(
            P(None, "ep", None),
            P("section", None, "ep", None),
            P("section"),
            P("section", None),
            P("section", None, None),
            P("section", None, "ep"),
            P("section", None, "ep"),
            P("section", "ep", None),
        ),
        out_specs=(P("section", None, "ep", None), P("section", "ep")),
        check_vma=False,
    )
```

```python
import functools

import jax
import jax.numpy as jnp
from jax import lax
from jax.experimental import pallas as pl
from jax.experimental.pallas import tpu as pltpu
from jax.sharding import PartitionSpec as P

FFW = 1024
BLK = 256
VM = pl.BlockSpec(memory_space=pltpu.VMEM)
SM = pl.BlockSpec(memory_space=pltpu.SMEM)
F32 = jnp.float32
BF16 = jnp.bfloat16


def live_hop(block, axis, tick, micro_count):
    last = lax.axis_size(axis) - 1
    route = [(s, s + 1) for s in range(last) if 0 <= tick - s < micro_count]
    return lax.ppermute(block, axis, route)


PACE = 1


def pacing(token, tick, micro_count):
    last = lax.axis_size("section") - 1
    done = tick + 1 - micro_count
    sections = [0] if tick + 1 < micro_count else [done] if done % 2 == 0 and done < last else []
    n = lax.axis_size("ep")
    pairs = [(s * n + p, s * n + (p ^ 1)) for s in sections for p in range(n)]
    for _ in range(PACE if pairs else 0):
        token = lax.ppermute(token, ("section", "ep"), pairs)
    return (token,) if pairs else ()


def busy(tick, micro_count):
    section = lax.axis_index("section")
    m = tick - section
    return (m >= 0) & (m < micro_count + 1 - section % 2)


def row_ids(rows, lanes, experts, capacity):
    row = lax.broadcasted_iota(jnp.int32, (rows, lanes), 1)
    return row // (lanes // experts), row // capacity % 2, row % capacity


def column(routes, k):
    tokens = routes.shape[1]
    shape = (tokens, tokens)
    same = lax.broadcasted_iota(jnp.int32, shape, 0) == lax.broadcasted_iota(jnp.int32, shape, 1)
    spread = jnp.broadcast_to(routes[k : k + 1].astype(F32), shape)
    return jnp.sum(jnp.where(same, spread, 0.0), axis=1, keepdims=True)


def plan(hot_ref, routes_ref, unpack_ref, info_ref):
    micro_count, top_count, tokens = routes_ref.shape
    lanes = unpack_ref.shape[2]
    expert, half_id, slot = row_ids(tokens, lanes, 8, tokens // 2)
    before = (
        lax.broadcasted_iota(jnp.int32, (tokens, tokens), 0)
        > lax.broadcasted_iota(jnp.int32, (tokens, tokens), 1)
    ).astype(BF16)
    counts = jnp.zeros((tokens, lanes), F32)
    for m in range(micro_count):
        ids = routes_ref[m]
        hit = jnp.zeros((tokens, lanes), F32)
        for k in range(top_count):
            hit = hit + (column(ids, k) == expert.astype(F32)).astype(F32)
        rank = jnp.dot(before, hit.astype(BF16), preferred_element_type=F32)
        placed = jnp.where(rank == slot.astype(F32), hit, 0.0)
        unpack_ref[m, :tokens] = jnp.where(half_id == 0, placed, 0.0)
        unpack_ref[m, tokens:] = jnp.where(half_id == 1, placed, 0.0)
        counts = counts + hit
    counts = jnp.sum(counts, axis=0, keepdims=True)
    hot = hot_ref[0]
    device = lax.axis_index("ep")
    lane = lax.broadcasted_iota(jnp.int32, counts.shape, 1)
    per = lanes // 8
    homes = 2.0 - (hot // 2 == device).astype(F32)
    info_ref[0:1] = jnp.where(lane == device // 2 * per, homes, 0.0)
    info_ref[1:2] = jnp.where(lane == hot // (FFW // BLK) * per, counts, 0.0)
    return counts


def pre_kernel(tick, *refs):
    if tick == 0:
        hot_ref, *sources, send_ref, mix_ref, input_ref, unpack_ref, info_ref = refs[:10]
        rows_ref, gain_ref, router_ref, routes_ref, sems = refs[10:]
        copies = [
            pltpu.make_async_copy(source, held, sems.at[i])
            for i, (source, held) in enumerate(zip(sources, refs[10:14]))
        ]
        for copy in copies:
            copy.start()
        for copy in copies:
            copy.wait()
    else:
        rows_ref, gain_ref, router_ref, routes_ref, unpack_ref, came_ref, *_, send_ref, mix_ref, input_ref = refs
    micro_count, tokens, width = rows_ref.shape
    half = width // 2
    section = lax.axis_index("section")
    m = jnp.clip(tick - section, 0, micro_count - 1)
    if tick == 0:
        counts = plan(hot_ref, routes_ref, unpack_ref, info_ref)
        send_ref[:, half:] = jnp.broadcast_to(
            counts, (send_ref.shape[0], counts.shape[1])
        ).astype(BF16)
        x = rows_ref[0]
    else:
        x = came_ref[...]
        if tick < micro_count:
            x = jnp.where(section == 0, rows_ref[tick].astype(F32), x.astype(F32)).astype(BF16)
    input_ref[...] = x
    x = x.astype(F32)
    mean_square = jnp.mean(x * x, axis=-1, keepdims=True)
    normed = x * lax.rsqrt(mean_square + 1e-06) * gain_ref[...]
    halves = jnp.concatenate([normed[:, :half], normed[:, half:]], axis=0).astype(BF16)
    unpack = unpack_ref[m]
    send_ref[:, :half] = lax.dot_general(
        unpack.astype(BF16), halves, (((0,), (0,)), ((), ())), preferred_element_type=F32
    ).astype(BF16)
    logits = lax.dot_general(
        normed.astype(BF16), router_ref[...], (((1,), (1,)), ((), ())), preferred_element_type=F32
    )
    experts = router_ref.shape[0]
    ids = routes_ref[m]
    expert = lax.broadcasted_iota(jnp.int32, (tokens, experts), 1)
    routed = jnp.zeros((tokens, experts), F32)
    for k in range(ids.shape[0]):
        routed = routed + (column(ids, k) == expert.astype(F32)).astype(F32)
    scores = routed / (1.0 + jnp.exp(-logits))
    gates = 2.5 * scores / jnp.sum(scores, axis=1, keepdims=True)
    owner = row_ids(tokens, unpack.shape[1], experts, tokens // 2)[0]
    wide = jnp.zeros(owner.shape, F32)
    for e in range(experts):
        wide = jnp.where(owner == e, gates[:, e : e + 1], wide)
    mix = jnp.concatenate([wide, wide], axis=0) * unpack
    high = mix.astype(BF16)
    mix_ref[: mix.shape[0]] = high
    mix_ref[mix.shape[0] :] = (mix - high.astype(F32)).astype(BF16)


def pre_or_idle(tick, micro_count, *refs):
    if tick == 0:
        pre_kernel(tick, *refs)
    else:

        @pl.when(busy(tick, micro_count))
        def _():
            pre_kernel(tick, *refs)


def product(rows_ref, gate_ref, up_ref, down_ref, out_ref, act_ref, arrived):
    count, half = out_ref.shape
    hidden = gate_ref.shape[1]
    left = rows_ref[:, :half]
    keep = lax.broadcasted_iota(jnp.int32, (count, 256), 0) % 8 < 4

    def joined(w_ref, cols):
        a = jnp.dot(left, w_ref[:half, cols], preferred_element_type=F32)
        b = jnp.dot(left, w_ref[half:, cols], preferred_element_type=F32)
        return a + pltpu.roll(b, count - 4, 0)

    for n in range(hidden // 256):
        cols = slice(n * 256, n * 256 + 256)
        arrived(2 * n)
        g = joined(gate_ref, cols)
        arrived(2 * n + 1)
        u = joined(up_ref, cols)
        act = g / (1.0 + jnp.exp(-g)) * u
        act = jnp.where(keep, act, 0.0)
        act_ref[:, cols] = act.astype(BF16)
        act_ref[:, n * 256 + hidden : n * 256 + hidden + 256] = pltpu.roll(act, 4, 0).astype(BF16)
    first = act_ref[:, :hidden]
    second = act_ref[:, hidden:]
    wide = half // 2
    for n in range(2):
        cols = slice(n * wide, n * wide + wide)
        rest = slice(half + n * wide, half + n * wide + wide)
        arrived(hidden // 128 + n)
        out = jnp.dot(first, down_ref[:, cols], preferred_element_type=F32) + jnp.dot(
            second, down_ref[:, rest], preferred_element_type=F32
        )
        out_ref[:, cols] = out.astype(BF16)


def expert_kernel(tick, micro_count, rows_ref, gate_ref, up_ref, down_ref, out_ref, act_ref):
    @pl.when(busy(tick, micro_count))
    def _():
        product(rows_ref, gate_ref, up_ref, down_ref, out_ref, act_ref, lambda step: None)


def first_kernel(info_ref, rows_ref, gate_hbm, up_hbm, down_hbm,
                 out_ref, load_ref, gate_ref, up_ref, down_ref, act_ref, sems):
    half = out_ref.shape[1]
    hidden = gate_ref.shape[1]
    wide = half // 2
    steps = []
    for n in range(hidden // 256):
        cols = slice(n * 256, n * 256 + 256)
        steps.append([(gate_hbm, gate_ref, cols)])
        steps.append([(up_hbm, up_ref, cols)])
    for n in range(2):
        steps.append(
            [(down_hbm, down_ref, slice(c + n * wide, c + n * wide + wide)) for c in (0, half)]
        )
    copies = []
    for step in steps:
        started = []
        for src, dst, cols in step:
            index = sum(map(len, copies)) + len(started)
            copy = pltpu.make_async_copy(src.at[:, cols], dst.at[:, cols], sems.at[index])
            copy.start()
            started.append(copy)
        copies.append(started)

    units = jnp.sum(rows_ref[:, half:].astype(F32), axis=0, keepdims=True) * 0.125
    load_ref[...] = jnp.broadcast_to(
        jnp.sum(units * info_ref[0:1] + info_ref[1:2], axis=1, keepdims=True) / 256.0, load_ref.shape
    )

    def arrived(step):
        for copy in copies[step]:
            copy.wait()

    live = lax.axis_index("section") == 0

    @pl.when(live)
    def _():
        product(rows_ref, gate_ref, up_ref, down_ref, out_ref, act_ref, arrived)

    @pl.when(jnp.logical_not(live))
    def _():
        for step in range(len(copies)):
            arrived(step)


def post_kernel(tick, x_ref, back_ref, mix_ref, *rest):
    out_ref, kept_ref = rest[-2:]
    half = back_ref.shape[1]
    tokens = x_ref.shape[0]
    both = jnp.dot(mix_ref[...], back_ref[...], preferred_element_type=F32)
    total = both[: 2 * tokens] + both[2 * tokens :]
    x = x_ref[...].astype(F32)
    left = (x[:, :half] + total[:tokens]).astype(BF16)
    right = (x[:, half:] + total[tokens:]).astype(BF16)
    out_ref[:, :half] = left
    out_ref[:, half:] = right
    m = tick - lax.axis_index("section")

    @pl.when((m >= 0) & (m < kept_ref.shape[0]))
    def _():
        kept_ref[m, :, :half] = left
        kept_ref[m, :, half:] = right


def local(rows_in, routes, hot_blocks, gains, router, w_gate, w_up, w_down):
    section_count = lax.axis_size("section")
    ep_count = lax.axis_size("ep")
    micro_count, tok_rows, model_width = rows_in.shape
    half = model_width // 2
    count = ep_count * tok_rows
    hidden = w_gate.shape[2]
    resident = functools.partial(pltpu.with_memory_space_constraint, memory_space=pltpu.VMEM)
    outside = functools.partial(pltpu.with_memory_space_constraint, memory_space=pltpu.HBM)
    HB = pl.BlockSpec(memory_space=pltpu.HBM)
    router_t = router[0].T
    routes_t = routes[0].transpose(0, 2, 1)
    row_shape = jax.ShapeDtypeStruct((tok_rows, model_width), BF16)

    def params(mib):
        return pltpu.CompilerParams(vmem_limit_bytes=mib << 20)

    def pre(tick, *more):
        out_shape = [
            jax.ShapeDtypeStruct((count, half + (count if tick == 0 else 0)), BF16),
            jax.ShapeDtypeStruct((4 * tok_rows, count), BF16),
            row_shape,
        ]
        if tick == 0:
            out_shape += [
                jax.ShapeDtypeStruct((micro_count, 2 * tok_rows, count), F32),
                jax.ShapeDtypeStruct((2, count), F32),
            ]
        values = (rows_in, gains, router_t, routes_t)
        if tick == 0:
            values = (hot_blocks, *map(outside, values))
            specs = [SM] + [HB] * 4
            scratch = [pltpu.VMEM(v.shape, v.dtype) for v in values[1:]]
            scratch += [pltpu.SemaphoreType.DMA((4,))]
        else:
            values += more
            specs = [VM] * len(values)
            scratch = []
        return pl.pallas_call(
            functools.partial(pre_or_idle, tick, micro_count),
            out_shape=out_shape,
            in_specs=specs,
            out_specs=[VM] * len(out_shape),
            scratch_shapes=scratch,
            compiler_params=params(8),
            name="pre",
        )(*values)

    part_shape = jax.ShapeDtypeStruct((count, half), BF16)
    act_shape = pltpu.VMEM((count, 2 * hidden), BF16)
    weights = (w_gate[0], w_up[0], w_down[0])

    def first(rows, info):
        return pl.pallas_call(
            first_kernel,
            out_shape=[part_shape, jax.ShapeDtypeStruct((1, 128), F32)]
            + [pltpu.VMEM(w.shape, w.dtype) for w in weights],
            in_specs=[VM, VM] + [HB] * 3,
            out_specs=[VM] * 5,
            scratch_shapes=[act_shape, pltpu.SemaphoreType.DMA((8,))],
            compiler_params=params(12),
            name="first",
        )(info, rows, *map(outside, weights))

    def experts(tick, rows, held):
        return pl.pallas_call(
            functools.partial(expert_kernel, tick, micro_count),
            out_shape=part_shape,
            in_specs=[VM] * 4,
            out_specs=VM,
            scratch_shapes=[act_shape],
            compiler_params=params(12),
            name="experts",
        )(rows, *map(resident, held))

    def post(tick, x, back, mix, *kept):
        return pl.pallas_call(
            functools.partial(post_kernel, tick),
            out_shape=(row_shape, pltpu.VMEM(rows_in.shape, BF16)),
            in_specs=[VM] * (3 + len(kept)),
            out_specs=(VM, VM),
            input_output_aliases={3: 1} if kept else {},
            compiler_params=params(8),
            name="post",
        )(x, back, mix, *map(resident, kept))

    def exchange(block):
        return lax.all_to_all(block, "ep", split_axis=0, concat_axis=0, tiled=True)

    kept = ()
    last = micro_count + section_count - 2
    for tick in range(last + 1):
        if tick == 0:
            send, mix, layer_input, unpack, info = pre(tick)
            part, relative, *held = first(exchange(send), info)
        else:
            send, mix, layer_input = pre(tick, unpack, incoming, *pace)
            part = experts(tick, exchange(send), held)
        next_rows, *kept = post(tick, layer_input, exchange(part), mix, *kept)
        if tick < last:
            incoming = live_hop(next_rows, "section", tick, micro_count)
            incoming, token = lax.optimization_barrier((incoming, mix))
            pace = pacing(token, tick, micro_count)
    return (kept[0][None], relative[:, :1])


def solution(mesh):
    return jax.shard_map(
        local,
        mesh=mesh,
        in_specs=(
            P(None, "ep", None),
            P("section", None, "ep", None),
            P("section"),
            P("section", None),
            P("section", None, None),
            P("section", None, "ep"),
            P("section", None, "ep"),
            P("section", "ep", None),
        ),
        out_specs=(P("section", None, "ep", None), P("section", "ep")),
        check_vma=False,
    )
```

```python
import functools

import jax
import jax.numpy as jnp
from jax import lax
from jax.experimental import pallas as pl
from jax.experimental.pallas import tpu as pltpu
from jax.sharding import PartitionSpec as P

FFW = 1024
BLK = 256
VM = pl.BlockSpec(memory_space=pltpu.VMEM)
SM = pl.BlockSpec(memory_space=pltpu.SMEM)
DOWN_PARTS = 7
F32 = jnp.float32
BF16 = jnp.bfloat16


def live_hop(block, axis, tick, micro_count):
    last = lax.axis_size(axis) - 1
    route = [(s, s + 1) for s in range(last) if 0 <= tick - s < micro_count]
    return lax.ppermute(block, axis, route)


PACE = 1


def pacing(token, tick, micro_count):
    last = lax.axis_size("section") - 1
    done = tick + 1 - micro_count
    sections = [0] if tick + 1 < micro_count else [done] if done % 2 == 0 and done < last else []
    n = lax.axis_size("ep")
    pairs = [(s * n + p, s * n + (p ^ 1)) for s in sections for p in range(n)]
    for _ in range(PACE if pairs else 0):
        token = lax.ppermute(token, ("section", "ep"), pairs)
    return (token,) if pairs else ()


def row_ids(rows, lanes, experts, capacity):
    row = lax.broadcasted_iota(jnp.int32, (rows, lanes), 1)
    return row // (lanes // experts), row // capacity % 2, row % capacity


def column(routes, k):
    tokens = routes.shape[1]
    shape = (tokens, tokens)
    same = lax.broadcasted_iota(jnp.int32, shape, 0) == lax.broadcasted_iota(jnp.int32, shape, 1)
    spread = jnp.broadcast_to(routes[k : k + 1].astype(F32), shape)
    return jnp.sum(jnp.where(same, spread, 0.0), axis=1, keepdims=True)


def plan(hot_ref, routes_ref, unpack_ref, info_ref):
    micro_count, top_count, tokens = routes_ref.shape
    lanes = unpack_ref.shape[2]
    expert, half_id, slot = row_ids(tokens, lanes, 8, tokens // 2)
    before = (
        lax.broadcasted_iota(jnp.int32, (tokens, tokens), 0)
        > lax.broadcasted_iota(jnp.int32, (tokens, tokens), 1)
    ).astype(BF16)
    counts = jnp.zeros((tokens, lanes), F32)
    for m in range(micro_count):
        ids = routes_ref[m]
        hit = jnp.zeros((tokens, lanes), F32)
        for k in range(top_count):
            hit = hit + (column(ids, k) == expert.astype(F32)).astype(F32)
        rank = jnp.dot(before, hit.astype(BF16), preferred_element_type=F32)
        placed = jnp.where(rank == slot.astype(F32), hit, 0.0)
        unpack_ref[m, :tokens] = jnp.where(half_id == 0, placed, 0.0)
        unpack_ref[m, tokens:] = jnp.where(half_id == 1, placed, 0.0)
        counts = counts + hit
    counts = jnp.sum(counts, axis=0, keepdims=True)
    hot = hot_ref[0]
    device = lax.axis_index("ep")
    lane = lax.broadcasted_iota(jnp.int32, counts.shape, 1)
    per = lanes // 8
    homes = 2.0 - (hot // 2 == device).astype(F32)
    info_ref[0:1] = jnp.where(lane == device // 2 * per, homes, 0.0)
    info_ref[1:2] = jnp.where(lane == hot // (FFW // BLK) * per, counts, 0.0)
    return counts


def pre_kernel(tick, *refs):
    if tick == 0:
        hot_ref, *sources, send_ref, mix_ref, input_ref, unpack_ref, info_ref = refs[:10]
        rows_ref, gain_ref, router_ref, routes_ref, sems = refs[10:]
        copies = [
            pltpu.make_async_copy(source, held, sems.at[i])
            for i, (source, held) in enumerate(zip(sources, refs[10:14]))
        ]
        for copy in copies:
            copy.start()
        for copy in copies:
            copy.wait()
    else:
        rows_ref, gain_ref, router_ref, routes_ref, unpack_ref, came_ref, *_, send_ref, mix_ref, input_ref = refs
    micro_count, tokens, width = rows_ref.shape
    half = width // 2
    section = lax.axis_index("section")
    m = jnp.clip(tick - section, 0, micro_count - 1)
    if tick == 0:
        counts = plan(hot_ref, routes_ref, unpack_ref, info_ref)
        send_ref[:, half:] = jnp.broadcast_to(
            counts, (send_ref.shape[0], counts.shape[1])
        ).astype(BF16)
        x = rows_ref[0]
    else:
        x = came_ref[...]
        if tick < micro_count:
            x = jnp.where(section == 0, rows_ref[tick].astype(F32), x.astype(F32)).astype(BF16)
    input_ref[...] = x
    x = x.astype(F32)
    mean_square = jnp.mean(x * x, axis=-1, keepdims=True)
    normed = x * lax.rsqrt(mean_square + 1e-06) * gain_ref[...]
    halves = jnp.concatenate([normed[:, :half], normed[:, half:]], axis=0).astype(BF16)
    unpack = unpack_ref[m]
    send_ref[:, :half] = lax.dot_general(
        unpack.astype(BF16), halves, (((0,), (0,)), ((), ())), preferred_element_type=F32
    ).astype(BF16)
    logits = lax.dot_general(
        normed.astype(BF16), router_ref[...], (((1,), (1,)), ((), ())), preferred_element_type=F32
    )
    experts = router_ref.shape[0]
    ids = routes_ref[m]
    expert = lax.broadcasted_iota(jnp.int32, (tokens, experts), 1)
    routed = jnp.zeros((tokens, experts), F32)
    for k in range(ids.shape[0]):
        routed = routed + (column(ids, k) == expert.astype(F32)).astype(F32)
    scores = routed / (1.0 + jnp.exp(-logits))
    gates = 2.5 * scores / jnp.sum(scores, axis=1, keepdims=True)
    owner = row_ids(tokens, unpack.shape[1], experts, tokens // 2)[0]
    wide = jnp.zeros(owner.shape, F32)
    for e in range(experts):
        wide = jnp.where(owner == e, gates[:, e : e + 1], wide)
    mix = jnp.concatenate([wide, wide], axis=0) * unpack
    high = mix.astype(BF16)
    mix_ref[: mix.shape[0]] = high
    mix_ref[mix.shape[0] :] = (mix - high.astype(F32)).astype(BF16)


def product(rows_ref, gate_ref, up_ref, down_ref, out_ref, act_ref, arrived):
    count, half = out_ref.shape
    hidden = gate_ref.shape[1]
    left = rows_ref[:, :half]
    keep = lax.broadcasted_iota(jnp.int32, (count, 256), 0) % 8 < 4

    def joined(w_ref, cols):
        a = jnp.dot(left, w_ref[:half, cols], preferred_element_type=F32)
        b = jnp.dot(left, w_ref[half:, cols], preferred_element_type=F32)
        return a + pltpu.roll(b, count - 4, 0)

    for n in range(hidden // 256):
        cols = slice(n * 256, n * 256 + 256)
        arrived(2 * n)
        g = joined(gate_ref, cols)
        arrived(2 * n + 1)
        u = joined(up_ref, cols)
        act = g / (1.0 + jnp.exp(-g)) * u
        act = jnp.where(keep, act, 0.0)
        act_ref[:, cols] = act.astype(BF16)
        act_ref[:, n * 256 + hidden : n * 256 + hidden + 256] = pltpu.roll(act, 4, 0).astype(BF16)
    first = act_ref[:, :hidden]
    second = act_ref[:, hidden:]
    wide = half // DOWN_PARTS
    for n in range(DOWN_PARTS):
        cols = slice(n * wide, n * wide + wide)
        rest = slice(half + n * wide, half + n * wide + wide)
        arrived(hidden // 128 + n)
        out = jnp.dot(first, down_ref[:, cols], preferred_element_type=F32) + jnp.dot(
            second, down_ref[:, rest], preferred_element_type=F32
        )
        out_ref[:, cols] = out.astype(BF16)


def busy(tick, micro_count):
    m = tick - lax.axis_index("section")
    return (m >= 0) & (m <= micro_count)


def expert_kernel(tick, micro_count, rows_ref, gate_ref, up_ref, down_ref, out_ref, act_ref):
    @pl.when(busy(tick, micro_count))
    def _():
        product(rows_ref, gate_ref, up_ref, down_ref, out_ref, act_ref, lambda step: None)


def first_kernel(info_ref, rows_ref, gate_hbm, up_hbm, down_hbm,
                 out_ref, load_ref, gate_ref, up_ref, down_ref, act_ref, sems):
    half = out_ref.shape[1]
    hidden = gate_ref.shape[1]
    wide = half // DOWN_PARTS
    steps = []
    for n in range(hidden // 256):
        cols = slice(n * 256, n * 256 + 256)
        steps.append([(gate_hbm, gate_ref, cols)])
        steps.append([(up_hbm, up_ref, cols)])
    for n in range(DOWN_PARTS):
        steps.append(
            [(down_hbm, down_ref, slice(c + n * wide, c + n * wide + wide)) for c in (0, half)]
        )
    copies = []
    for step in steps:
        started = []
        for src, dst, cols in step:
            index = sum(map(len, copies)) + len(started)
            copy = pltpu.make_async_copy(src.at[:, cols], dst.at[:, cols], sems.at[index])
            copy.start()
            started.append(copy)
        copies.append(started)

    units = jnp.sum(rows_ref[:, half:].astype(F32), axis=0, keepdims=True) * 0.125
    load_ref[...] = jnp.broadcast_to(
        jnp.sum(units * info_ref[0:1] + info_ref[1:2], axis=1, keepdims=True) / 256.0, load_ref.shape
    )

    def arrived(step):
        for copy in copies[step]:
            copy.wait()

    product(rows_ref, gate_ref, up_ref, down_ref, out_ref, act_ref, arrived)


def post_kernel(tick, x_ref, back_ref, mix_ref, *rest):
    out_ref, kept_ref = rest[-2:]
    half = back_ref.shape[1]
    tokens = x_ref.shape[0]
    both = jnp.dot(mix_ref[...], back_ref[...], preferred_element_type=F32)
    total = both[: 2 * tokens] + both[2 * tokens :]
    x = x_ref[...].astype(F32)
    left = (x[:, :half] + total[:tokens]).astype(BF16)
    right = (x[:, half:] + total[tokens:]).astype(BF16)
    out_ref[:, :half] = left
    out_ref[:, half:] = right
    m = tick - lax.axis_index("section")

    @pl.when((m >= 0) & (m < kept_ref.shape[0]))
    def _():
        kept_ref[m, :, :half] = left
        kept_ref[m, :, half:] = right


def local(rows_in, routes, hot_blocks, gains, router, w_gate, w_up, w_down):
    section_count = lax.axis_size("section")
    ep_count = lax.axis_size("ep")
    micro_count, tok_rows, model_width = rows_in.shape
    half = model_width // 2
    count = ep_count * tok_rows
    hidden = w_gate.shape[2]
    resident = functools.partial(pltpu.with_memory_space_constraint, memory_space=pltpu.VMEM)
    outside = functools.partial(pltpu.with_memory_space_constraint, memory_space=pltpu.HBM)
    HB = pl.BlockSpec(memory_space=pltpu.HBM)
    router_t = router[0].T
    routes_t = routes[0].transpose(0, 2, 1)
    row_shape = jax.ShapeDtypeStruct((tok_rows, model_width), BF16)

    def params(mib):
        return pltpu.CompilerParams(vmem_limit_bytes=mib << 20)

    def pre(tick, *more):
        out_shape = [
            jax.ShapeDtypeStruct((count, half + (count if tick == 0 else 0)), BF16),
            jax.ShapeDtypeStruct((4 * tok_rows, count), BF16),
            row_shape,
        ]
        if tick == 0:
            out_shape += [
                jax.ShapeDtypeStruct((micro_count, 2 * tok_rows, count), F32),
                jax.ShapeDtypeStruct((2, count), F32),
            ]
        values = (rows_in, gains, router_t, routes_t)
        if tick == 0:
            values = (hot_blocks, *map(outside, values))
            specs = [SM] + [HB] * 4
            scratch = [pltpu.VMEM(v.shape, v.dtype) for v in values[1:]]
            scratch += [pltpu.SemaphoreType.DMA((4,))]
        else:
            values += more
            specs = [VM] * len(values)
            scratch = []
        return pl.pallas_call(
            functools.partial(pre_kernel, tick),
            out_shape=out_shape,
            in_specs=specs,
            out_specs=[VM] * len(out_shape),
            scratch_shapes=scratch,
            compiler_params=params(8),
            name="pre",
        )(*values)

    part_shape = jax.ShapeDtypeStruct((count, half), BF16)
    act_shape = pltpu.VMEM((count, 2 * hidden), BF16)
    weights = (w_gate[0], w_up[0], w_down[0])

    def first(rows, info):
        return pl.pallas_call(
            first_kernel,
            out_shape=[part_shape, jax.ShapeDtypeStruct((1, 128), F32)]
            + [pltpu.VMEM(w.shape, w.dtype) for w in weights],
            in_specs=[VM, VM] + [HB] * 3,
            out_specs=[VM] * 5,
            scratch_shapes=[act_shape, pltpu.SemaphoreType.DMA((2 * hidden // 256 + 2 * DOWN_PARTS,))],
            compiler_params=params(12),
            name="first",
        )(info, rows, *map(outside, weights))

    def experts(tick, rows, held):
        return pl.pallas_call(
            functools.partial(expert_kernel, tick, micro_count),
            out_shape=part_shape,
            in_specs=[VM] * 4,
            out_specs=VM,
            scratch_shapes=[act_shape],
            compiler_params=params(12),
            name="experts",
        )(rows, *map(resident, held))

    def post(tick, x, back, mix, *kept):
        return pl.pallas_call(
            functools.partial(post_kernel, tick),
            out_shape=(row_shape, pltpu.VMEM(rows_in.shape, BF16)),
            in_specs=[VM] * (3 + len(kept)),
            out_specs=(VM, VM),
            input_output_aliases={3: 1} if kept else {},
            compiler_params=params(8),
            name="post",
        )(x, back, mix, *map(resident, kept))

    def exchange(block):
        return lax.all_to_all(block, "ep", split_axis=0, concat_axis=0, tiled=True)

    kept = ()
    last = micro_count + section_count - 2
    for tick in range(last + 1):
        if tick == 0:
            send, mix, layer_input, unpack, info = pre(tick)
            part, relative, *held = first(exchange(send), info)
        else:
            send, mix, layer_input = pre(tick, unpack, incoming, *pace)
            part = experts(tick, exchange(send), held)
        next_rows, *kept = post(tick, layer_input, exchange(part), mix, *kept)
        if tick < last:
            incoming = live_hop(next_rows, "section", tick, micro_count)
            incoming, token = lax.optimization_barrier((incoming, mix))
            pace = pacing(token, tick, micro_count)
    return (kept[0][None], relative[:, :1])


def solution(mesh):
    return jax.shard_map(
        local,
        mesh=mesh,
        in_specs=(
            P(None, "ep", None),
            P("section", None, "ep", None),
            P("section"),
            P("section", None),
            P("section", None, None),
            P("section", None, "ep"),
            P("section", None, "ep"),
            P("section", "ep", None),
        ),
        out_specs=(P("section", None, "ep", None), P("section", "ep")),
        check_vma=False,
    )
```
